32 devices in a mesh: seq: 8 (over y, x, core), head: 4 (over z).
Axes of the slice: x: 2, y: 2, z: 4, core: 2. Of those that a mesh axis runs over, the one named last changes fastest.
Arguments:
- tokens: float32 [16384, 1024], P('seq'), may hold values from -6 to 6
- cotangent: float32 [16384, 1024], P('seq'), may hold values from -6 to 6
- sequence_starts: int32 [8], P('seq'), may hold values from 1 to 2048, as said below
- norm_gain: float32 [1024], replicated, may hold values from 0.5 to 1.5
- inner_weight: float32 [1024, 2, 2048], P('seq', None, 'head'), may hold values from -0.1875 to 0.1875
- state_weight: float32 [1024, 2, 128], P('seq', None, 'head'), may hold values from -0.1875 to 0.1875
- step_weight: float32 [1024, 32], P('seq', 'head'), may hold values from -0.1875 to 0.1875
- inner_params: float32 [6, 2048], P(None, 'head'), may hold values from -5 to 5
- state_conv: float32 [5, 2, 128], P(None, None, 'head'), may hold values from -3 to 3
- head_params: float32 [3, 32], P(None, 'head'), may hold values from -16 to 6
- output_weight: float32 [2048, 1024], P('head', 'seq'), may hold values from -0.125 to 0.125
- first_norm_gain: float32 [1024], replicated, may hold values from -768 to 768
- second_norm_gain: float32 [1024], replicated, may hold values from 16384 to 65536
- first_inner_weight: float32 [1024, 2, 2048], P('seq', None, 'head'), may hold values from -384 to 384
- second_inner_weight: float32 [1024, 2, 2048], P('seq', None, 'head'), may hold values from 4096 to 16384
- first_state_weight: float32 [1024, 2, 128], P('seq', None, 'head'), may hold values from -384 to 384
- second_state_weight: float32 [1024, 2, 128], P('seq', None, 'head'), may hold values from 4096 to 16384
- first_step_weight: float32 [1024, 32], P('seq', 'head'), may hold values from -384 to 384
- second_step_weight: float32 [1024, 32], P('seq', 'head'), may hold values from 4096 to 16384
- first_inner_params: float32 [6, 2048], P(None, 'head'), may hold values from -768 to 768
- second_inner_params: float32 [6, 2048], P(None, 'head'), may hold values from 16384 to 65536
- first_state_conv: float32 [5, 2, 128], P(None, None, 'head'), may hold values from -768 to 768
- second_state_conv: float32 [5, 2, 128], P(None, None, 'head'), may hold values from 16384 to 65536
- first_head_params: float32 [3, 32], P(None, 'head'), may hold values from -3072 to 3072
- second_head_params: float32 [3, 32], P(None, 'head'), may hold values from 262144 to 1048576
- first_output_weight: float32 [2048, 1024], P('head', 'seq'), may hold values from -768 to 768
- second_output_weight: float32 [2048, 1024], P('head', 'seq'), may hold values from 16384 to 65536
Outputs:
- output: float32 [16384, 1024], P('seq')
- input_gradient: float32 [16384, 1024], P('seq')
- next_norm_gain: float32 [1024], replicated
- next_first_norm_gain: float32 [1024], replicated
- next_second_norm_gain: float32 [1024], replicated
- next_inner_weight: float32 [1024, 2, 2048], P('seq', None, 'head')
- next_first_inner_weight: float32 [1024, 2, 2048], P('seq', None, 'head')
- next_second_inner_weight: float32 [1024, 2, 2048], P('seq', None, 'head')
- next_state_weight: float32 [1024, 2, 128], P('seq', None, 'head')
- next_first_state_weight: float32 [1024, 2, 128], P('seq', None, 'head')
- next_second_state_weight: float32 [1024, 2, 128], P('seq', None, 'head')
- next_step_weight: float32 [1024, 32], P('seq', 'head')
- next_first_step_weight: float32 [1024, 32], P('seq', 'head')
- next_second_step_weight: float32 [1024, 32], P('seq', 'head')
- next_inner_params: float32 [6, 2048], P(None, 'head')
- next_first_inner_params: float32 [6, 2048], P(None, 'head')
- next_second_inner_params: float32 [6, 2048], P(None, 'head')
- next_state_conv: float32 [5, 2, 128], P(None, None, 'head')
- next_first_state_conv: float32 [5, 2, 128], P(None, None, 'head')
- next_second_state_conv: float32 [5, 2, 128], P(None, None, 'head')
- next_head_params: float32 [3, 32], P(None, 'head')
- next_first_head_params: float32 [3, 32], P(None, 'head')
- next_second_head_params: float32 [3, 32], P(None, 'head')
- next_output_weight: float32 [2048, 1024], P('head', 'seq')
- next_first_output_weight: float32 [2048, 1024], P('head', 'seq')
- next_second_output_weight: float32 [2048, 1024], P('head', 'seq')
The draws below stay inside these ranges and needn't reach their ends.
Inputs may be any that keep to these rules, and one draw needn't show every extreme that they name: `sequence_starts`: entry k is the offset within the k-th block of 2048 tokens at which a new sequence begins, or 2048 where none begins there; the stream also begins a sequence at token 0. New sequences begin only in the first and the last block, so one sequence runs from the first block to the last.
All inputs are finite; a program needn't handle non-finite values.
Results may differ from the reference program's by a relative error of at most 0.0015.
The reference program's roundings to bfloat16 on the way count: a program that leaves them out, or rounds other values in their place, can miss the bound.
Values may be sent and summed in bfloat16 or wider, within the bound.
No kernel may reach another device: no remote copies, remote signals or barrier semaphores. Data moves between devices by JAX's collectives and lax.ppermute only.
A program may use at most 192 MiB of HBM per device.

```python
import math
import jax
import jax.numpy as jnp
from jax import lax

D = 1024
HEADS = 32
HEADDIM = 64
STATE = 128
CONV = 4
BLOCK = 256
STEP = 10
TOK_DEV = 2048
INNER = 2048
TOKENS = 16384
N_SEQ = 8


def draw_sequence_starts(key, part):
    key = jax.random.fold_in(key, 1)
    first_key, final_key = jax.random.split(key, 2)
    first = jax.random.randint(first_key, (), 1, TOK_DEV, jnp.int32)
    final = jax.random.randint(final_key, (), 1, TOK_DEV, jnp.int32)
    starts = jnp.full((N_SEQ,), TOK_DEV, jnp.int32)
    return starts.at[0].set(first).at[N_SEQ - 1].set(final)


def draw_head_params(key, part):
    key = jax.random.fold_in(key, 2)
    pick_key, bias_key, rate_key, skip_key = jax.random.split(key, 4)
    fast_share = 0.4
    fast = jax.random.uniform(pick_key, (HEADS,), jnp.float32) < fast_share
    bias_jitter = jax.random.uniform(bias_key, (HEADS,), jnp.float32, -0.5, 0.5)
    rate_jitter = jax.random.uniform(rate_key, (HEADS,), jnp.float32, -0.5, 0.5)
    half_log = 0.5 * jnp.log(jnp.float32(TOKENS))
    step_bias = jnp.where(fast, -0.5 + bias_jitter, 1.386 - half_log + bias_jitter)
    log_rate = jnp.where(fast, -3.5 + rate_jitter, -1.89 - half_log + rate_jitter)
    skip = jax.random.uniform(skip_key, (HEADS,), jnp.float32, 2.0, 6.0)
    return jnp.stack([step_bias, log_rate, skip], axis=0)


def draw_inner_params(key, part):
    key = jax.random.fold_in(key, 3)
    tap_key, bias_key, gain_key = jax.random.split(key, 3)
    column = jnp.arange(INNER, dtype=jnp.float32) / (INNER - 1)
    rise = jnp.sqrt(1.0 + 2.0 * column)
    taps = jnp.clip(jax.random.normal(tap_key, (CONV, INNER), jnp.float32), -4.0, 4.0) * 0.5 * rise
    bias = jnp.clip(jax.random.normal(bias_key, (1, INNER), jnp.float32), -4.0, 4.0) * 0.3
    gain = jax.random.uniform(gain_key, (1, INNER), jnp.float32, 0.7, 1.3)
    return jnp.concatenate([taps, bias, gain], axis=0)


def strengthened(array, own_key, source, target, parts, factor):
    def block_of(position):
        return (jnp.arange(array.shape[position]) // (array.shape[position] // parts)).reshape((-1,) + (1,) * (array.ndim - 1 - position))

    near = jax.random.permutation(own_key, parts)[block_of(target)]
    other_side = (block_of(target) + parts // 2) % parts
    return jnp.where((block_of(source) == near) | (block_of(source) == other_side), factor * array, array)


def levels(key, shape, cuts, low, top_value):
    level, own = 1.0, jax.random.fold_in(key, 6)
    for axis_at, parts in cuts:
        heights = jnp.exp(jax.random.uniform(jax.random.fold_in(own, axis_at), (parts,), jnp.float32, low / len(cuts), top_value / len(cuts)))
        level = level * jnp.repeat(heights, shape[axis_at] // parts).reshape([-1 if axis == axis_at else 1 for axis in range(len(shape))])
    return level


def gaussian(own_key, extent, width, limit, pieces=(), held_as=jnp.bfloat16):
    values = jax.random.normal(own_key, extent, jnp.float32) * width
    if len(pieces) > 0:
        values = levels(own_key, extent, pieces, -0.22, 0.18) * values
    return jnp.clip(values, min=-limit, max=limit).astype(held_as)


def gaussian_with(stream_key, shape, deviation, reach, pieces, heavy, kind=jnp.bfloat16):
    result = deviation * jax.random.normal(stream_key, shape, jnp.float32)
    if pieces:
        result = result * levels(stream_key, shape, pieces, -0.22, 0.18)
    return jnp.clip(strengthened(result, jax.random.fold_in(stream_key, 3), *heavy), -reach, reach).astype(kind)


def setup_inputs(seed: int = 0) -> dict:
    arg_keys = jax.random.split(jax.random.key(seed), 28)
    return {
        "tokens": gaussian_with(arg_keys[0], (TOKENS, D), 1.0, 6.0, ((0, 8),), (0, 1, 8, 2.0), jnp.float32),
        "cotangent": gaussian_with(arg_keys[1], (TOKENS, D), 1.0, 6.0, ((0, 8),), (0, 1, 8, 2.0), jnp.float32),
        "sequence_starts": draw_sequence_starts(jax.random.fold_in(arg_keys[27], 71), 0),
        "norm_gain": jnp.clip(1.0 + 0.1 * jax.random.normal(arg_keys[3], (D,), jnp.float32), 0.5, 1.5),
        "inner_weight": gaussian(arg_keys[4], (D, 2, INNER), D ** -0.5, 0.1875, ((0, 8), (2, 4)), jnp.float32),
        "state_weight": gaussian(arg_keys[5], (D, 2, STATE), D ** -0.5, 0.1875, ((0, 8), (2, 4)), jnp.float32),
        "step_weight": gaussian(arg_keys[6], (D, HEADS), D ** -0.5, 0.1875, ((0, 8), (1, 4)), jnp.float32),
        "inner_params": draw_inner_params(jax.random.fold_in(arg_keys[27], 71), 0),
        "state_conv": gaussian(arg_keys[8], (CONV + 1, 2, STATE), 0.5, 3.0, ((2, 4),), jnp.float32),
        "head_params": draw_head_params(jax.random.fold_in(arg_keys[27], 71), 0),
        "output_weight": gaussian(arg_keys[10], (INNER, D), INNER ** -0.5, 0.125, ((0, 4), (1, 8)), jnp.float32),
        "first_norm_gain": gaussian(arg_keys[11], (D,), (TOKENS ** 0.5), 768.0, (), jnp.float32),
        "second_norm_gain": jnp.clip(jnp.exp(jax.random.uniform(arg_keys[12], (D,), jnp.float32, math.log(16384.0), math.log(65536.0))), 16384.0, 65536.0),
        "first_inner_weight": gaussian(arg_keys[13], (D, 2, INNER), (0.5 * TOKENS ** 0.5), 384.0, ((0, 8), (2, 4)), jnp.float32),
        "second_inner_weight": jnp.clip(jnp.exp(math.log(16384.0) - 1.3862944 * jax.random.uniform(arg_keys[14], (D, 2, INNER), jnp.float32) ** levels(arg_keys[14], (D, 2, INNER), ((0, 8), (2, 4)), -0.2, 0.2)), 4096.0, 16384.0),
        "first_state_weight": gaussian(arg_keys[15], (D, 2, STATE), (0.5 * TOKENS ** 0.5), 384.0, ((0, 8), (2, 4)), jnp.float32),
        "second_state_weight": jnp.clip(jnp.exp(math.log(16384.0) - 1.3862944 * jax.random.uniform(arg_keys[16], (D, 2, STATE), jnp.float32) ** levels(arg_keys[16], (D, 2, STATE), ((0, 8), (2, 4)), -0.2, 0.2)), 4096.0, 16384.0),
        "first_step_weight": gaussian(arg_keys[17], (D, HEADS), (0.5 * TOKENS ** 0.5), 384.0, ((0, 8), (1, 4)), jnp.float32),
        "second_step_weight": jnp.clip(jnp.exp(math.log(16384.0) - 1.3862944 * jax.random.uniform(arg_keys[18], (D, HEADS), jnp.float32) ** levels(arg_keys[18], (D, HEADS), ((0, 8), (1, 4)), -0.2, 0.2)), 4096.0, 16384.0),
        "first_inner_params": gaussian(arg_keys[19], (CONV + 2, INNER), (TOKENS ** 0.5), 768.0, ((1, 4),), jnp.float32),
        "second_inner_params": jnp.clip(jnp.exp(math.log(65536.0) - 1.3862944 * jax.random.uniform(arg_keys[20], (CONV + 2, INNER), jnp.float32) ** levels(arg_keys[20], (CONV + 2, INNER), ((1, 4),), -0.2, 0.2)), 16384.0, 65536.0),
        "first_state_conv": gaussian(arg_keys[21], (CONV + 1, 2, STATE), (TOKENS ** 0.5), 768.0, ((2, 4),), jnp.float32),
        "second_state_conv": jnp.clip(jnp.exp(math.log(65536.0) - 1.3862944 * jax.random.uniform(arg_keys[22], (CONV + 1, 2, STATE), jnp.float32) ** levels(arg_keys[22], (CONV + 1, 2, STATE), ((2, 4),), -0.2, 0.2)), 16384.0, 65536.0),
        "first_head_params": gaussian(arg_keys[23], (3, HEADS), (4 * TOKENS ** 0.5), 3072.0, ((1, 4),), jnp.float32),
        "second_head_params": jnp.clip(jnp.exp(math.log(1048576) - 1.3862944 * jax.random.uniform(arg_keys[24], (3, HEADS), jnp.float32) ** levels(arg_keys[24], (3, HEADS), ((1, 4),), -0.2, 0.2)), 262144.0, 1048576),
        "first_output_weight": gaussian(arg_keys[25], (INNER, D), (TOKENS ** 0.5), 768.0, ((0, 4), (1, 8)), jnp.float32),
        "second_output_weight": jnp.clip(jnp.exp(math.log(65536.0) - 1.3862944 * jax.random.uniform(arg_keys[26], (INNER, D), jnp.float32) ** levels(arg_keys[26], (INNER, D), ((0, 4), (1, 8)), -0.2, 0.2)), 16384.0, 65536.0),
    }


@jax.custom_vjp
def low(v):
    return lax.optimization_barrier(v.astype(jnp.bfloat16)).astype(jnp.float32)

@jax.custom_vjp
def low_back(v):
    return v

def low_keep(v):
    return (low(v), None)

def low_pass(kept, grad):
    return (grad,)

def back_keep(v):
    return (v, None)

def back_low(kept, grad):
    return (low(grad),)
low.defvjp(low_keep, low_pass)
low_back.defvjp(back_keep, back_low)
norm_epsilon = 1e-05
adam_epsilon = 1e-08
moment_decay = 0.5
weight_decay = 0.1
highest = lax.Precision.HIGHEST

def matmul(left, right):
    return jnp.dot(left, right, precision=highest, preferred_element_type=jnp.float32)

def segment_ids(sequence_starts):
    device = jnp.arange(N_SEQ, dtype=jnp.int32)
    begins = jnp.where(sequence_starts < TOK_DEV, device * TOK_DEV + sequence_starts, TOKENS)
    places = jnp.arange(TOKENS, dtype=jnp.int32)
    return lax.optimization_barrier(jnp.sum((begins[None, :] <= places[:, None]).astype(jnp.int32), axis=1)).astype(jnp.int32)

def causal_conv(conv_in, taps, segments):
    padded = jnp.concatenate([jnp.zeros((CONV - 1, conv_in.shape[1]), jnp.float32), conv_in], axis=0)
    padded_segments = jnp.concatenate([jnp.zeros((CONV - 1,), jnp.int32), segments])
    total = jnp.broadcast_to(taps[CONV], conv_in.shape)
    for offset in range(CONV):
        match = (padded_segments[offset:offset + TOKENS] == segments).astype(jnp.float32)
        total = total + taps[offset] * padded[offset:offset + TOKENS] * match[:, None]
    return total

def block_scan(carry, block):
    state_in, segment_in = carry
    values, steps, logdecay, keys, queries, segments = block
    cumulative = jnp.cumsum(logdecay, axis=0)
    order = jnp.arange(BLOCK)
    same = (segments[:, None] == segments[None, :]) & (order[:, None] >= order[None, :])
    spread = cumulative[:, None, :] - cumulative[None, :, :]
    decay = jnp.where(same[:, :, None], jnp.exp(jnp.where(same[:, :, None], spread, 0.0)), 0.0)
    scores = matmul(queries, keys.T)
    mixing = scores[:, :, None] * decay * steps[None, :, :]
    inner = jnp.einsum('ijh,jhp->ihp', mixing, values, precision=highest)
    keep = (segments == segment_in).astype(jnp.float32)
    carried = jnp.einsum('in,hpn->ihp', queries, state_in, precision=highest) * (jnp.exp(cumulative) * keep[:, None])[:, :, None]
    ending = (segments == segments[-1]).astype(jnp.float32)
    weights_end = jnp.exp(cumulative[-1][None, :] - cumulative) * ending[:, None] * steps
    state_out = (jnp.exp(cumulative[-1]) * keep[-1])[:, None, None] * state_in
    state_out = state_out + jnp.einsum('jh,jhp,jn->hpn', weights_end, values, keys, precision=highest)
    return ((state_out, segments[-1]), inner + carried)

def forward(tokens, norm_gain, inner_weight, state_weight, step_weight, inner_params, state_conv, head_params, output_weight, segments):
    variance = lax.optimization_barrier(jnp.mean(tokens * tokens, axis=1, keepdims=True))
    normed = tokens * lax.rsqrt(variance + norm_epsilon) * norm_gain
    rounded = low(normed)
    gates_values = low_back(matmul(rounded, low(inner_weight).reshape(D, 2 * INNER)))
    gates = gates_values[:, :INNER]
    values_in = gates_values[:, INNER:]
    state_in = low_back(matmul(rounded, low(state_weight).reshape(D, 2 * STATE)))
    raw_steps = low_back(matmul(rounded, low(step_weight)))
    conv_in = low(jnp.concatenate([values_in, state_in], axis=1))
    taps = jnp.concatenate([inner_params[:CONV + 1], state_conv.reshape(CONV + 1, 2 * STATE)], axis=1)
    activated = jax.nn.silu(causal_conv(conv_in, taps, segments))
    values = activated[:, :INNER]
    keys_queries = low(activated[:, INNER:])
    keys = keys_queries[:, :STATE]
    queries = keys_queries[:, STATE:]
    steps = jax.nn.softplus(raw_steps + head_params[0])
    logdecay = -jnp.exp(head_params[1]) * steps
    heads_values = values.reshape(TOKENS, HEADS, HEADDIM)
    count = TOKENS // BLOCK
    blocks = (heads_values.reshape(count, BLOCK, HEADS, HEADDIM), steps.reshape(count, BLOCK, HEADS), logdecay.reshape(count, BLOCK, HEADS), keys.reshape(count, BLOCK, STATE), queries.reshape(count, BLOCK, STATE), segments.reshape(count, BLOCK))
    start = (jnp.zeros((HEADS, HEADDIM, STATE), jnp.float32), jnp.zeros((), jnp.int32))
    ignored, mixed = lax.scan(jax.checkpoint(block_scan), start, blocks)
    mixed = mixed.reshape(TOKENS, HEADS, HEADDIM) + head_params[2][None, :, None] * heads_values
    gated = mixed.reshape(TOKENS, INNER) * jax.nn.silu(gates)
    gate_scale = lax.rsqrt(lax.optimization_barrier(jnp.mean(gated * gated, axis=1, keepdims=True)) + norm_epsilon)
    gate_out = low(gated * gate_scale * inner_params[CONV + 1])
    branch = low_back(matmul(gate_out, low(output_weight)))
    return tokens + branch

def adamw(weight, gradient, first, second, rate, shrink):
    first_new = moment_decay * first + (1.0 - moment_decay) * gradient
    second_new = moment_decay * second + (1.0 - moment_decay) * gradient * gradient
    correction = 1.0 - moment_decay ** STEP
    ratio = first_new / correction / (jnp.sqrt(second_new / correction) + adam_epsilon)
    return (weight - rate * (ratio + shrink * weight), first_new, second_new)

def reference(tokens, cotangent, sequence_starts, norm_gain, inner_weight, state_weight, step_weight, inner_params, state_conv, head_params, output_weight, first_norm_gain, second_norm_gain, first_inner_weight, second_inner_weight, first_state_weight, second_state_weight, first_step_weight, second_step_weight, first_inner_params, second_inner_params, first_state_conv, second_state_conv, first_head_params, second_head_params, first_output_weight, second_output_weight):
    segments = segment_ids(sequence_starts)

    def apply(tokens_in, gain_in, inner_in, state_in, step_in, params_in, conv_in, head_in, output_in):
        return forward(tokens_in, gain_in, inner_in, state_in, step_in, params_in, conv_in, head_in, output_in, segments)
    output, pullback = jax.vjp(apply, tokens, norm_gain, inner_weight, state_weight, step_weight, inner_params, state_conv, head_params, output_weight)
    grads = pullback(cotangent)
    matrix_rate = 2.0 * D ** (-0.5)
    output_rate = 2.0 * INNER ** (-0.5)
    gain_next = adamw(norm_gain, grads[1], first_norm_gain, second_norm_gain, 0.5, 0.0)
    inner_next = adamw(inner_weight, grads[2], first_inner_weight, second_inner_weight, matrix_rate, weight_decay)
    state_next = adamw(state_weight, grads[3], first_state_weight, second_state_weight, matrix_rate, weight_decay)
    step_next = adamw(step_weight, grads[4], first_step_weight, second_step_weight, matrix_rate, weight_decay)
    params_next = adamw(inner_params, grads[5], first_inner_params, second_inner_params, 0.5, 0.0)
    conv_next = adamw(state_conv, grads[6], first_state_conv, second_state_conv, 0.5, 0.0)
    head_next = adamw(head_params, grads[7], first_head_params, second_head_params, 3.0, 0.0)
    output_next = adamw(output_weight, grads[8], first_output_weight, second_output_weight, output_rate, weight_decay)
    return (output, grads[0], gain_next[0], gain_next[1], gain_next[2], inner_next[0], inner_next[1], inner_next[2], state_next[0], state_next[1], state_next[2], step_next[0], step_next[1], step_next[2], params_next[0], params_next[1], params_next[2], conv_next[0], conv_next[1], conv_next[2], head_next[0], head_next[1], head_next[2], output_next[0], output_next[1], output_next[2])
```

```python
import functools

import jax
import jax.numpy as jnp
from jax import lax
from jax.experimental import pallas as pl
from jax.experimental.pallas import tpu as pltpu
from jax.sharding import PartitionSpec as P

D = 1024
STATE = 128
CONV = 4
STEP = 10
INNER = 2048


norm_epsilon = 1e-05
adam_epsilon = 1e-08
moment_decay = 0.5
weight_decay = 0.1


def passed_along(value, axis, steps):
    count = lax.axis_size(axis)
    first, last = (max(0, -steps), min(count, count - steps))
    return lax.ppermute(value, axis, [(source, source + steps) for source in range(first, last)])


def carried_in(part, axis, reverse):
    count = lax.axis_size(axis)
    place = lax.axis_index(axis)
    parts = lax.all_gather(part, axis)
    states, decays = parts[:, :STATE], parts[:, STATE : STATE + 1]
    total = jnp.zeros_like(states[0])
    scale = jnp.ones_like(decays[0])
    for source in range(count) if reverse else reversed(range(count)):
        ahead = source > place if reverse else source < place
        total = total + jnp.where(ahead, scale, 0.0) * states[source]
        scale = scale * jnp.where(ahead, decays[source], 1.0)
    return total


def packed(block):
    top = jnp.max(jnp.abs(block), axis=0, keepdims=True)
    power = jnp.ceil(jnp.log2(jnp.maximum(top, 1e-30)))
    scaled = (block * jnp.exp2(14.0 - power)).astype(jnp.float16)
    note = jnp.broadcast_to(power, (16, block.shape[1])).astype(jnp.float16)
    return jnp.concatenate([scaled, note], axis=0)


def unpacked(message, zero=0.0):
    power = message[..., -16:-15, :].astype(jnp.float32) + zero
    return message[..., :-16, :].astype(jnp.float32) * jnp.exp2(power - 14.0)


def nothing(*others):
    total = jnp.float32(0.0)
    for other in others:
        first = lax.slice(other, (0,) * other.ndim, (1,) * other.ndim).reshape(())
        total = total + jnp.minimum(jnp.abs(first.astype(jnp.float32)), 0.0)
    return total


def halves_given(block, axis, bit):
    count = lax.axis_size(axis)
    upper = (lax.axis_index(axis) // bit) % 2
    half = block.shape[0] // 2
    kept = lax.dynamic_slice_in_dim(block, upper * half, half, 0)
    given = lax.dynamic_slice_in_dim(block, (1 - upper) * half, half, 0)
    pairs = [(place, place ^ bit) for place in range(count)]
    message = packed(given)
    return kept, message, lax.ppermute(message, axis, pairs)


def halves_joined(messages, axis, bit):
    count = lax.axis_size(axis)
    upper = (lax.axis_index(axis) // bit) % 2
    pairs = [(place, place ^ bit) for place in range(count)]
    other = lax.ppermute(messages, axis, pairs)
    return jnp.where(
        upper == 1,
        jnp.concatenate([other, messages], axis=0),
        jnp.concatenate([messages, other], axis=0),
    )


def halving_orders(axis):
    powers = [1 << power for power in range(lax.axis_size(axis).bit_length() - 1)]
    return powers, powers[::-1]


def reversed_bits(place, count):
    return sum((place // bit) % 2 * (count // (2 * bit)) for bit in halving_bits(count))


def halving_bits(count):
    return [1 << power for power in range(count.bit_length() - 1)]


class LineSum:
    def __init__(self, block, axis):
        self.axis = axis
        self.orders = halving_orders(axis)
        self.levels = len(self.orders[0])
        self.parts = list(jnp.split(block, 2))
        self.flight = None

    def send(self, level):
        sent = [
            halves_given(part, self.axis, order[level])
            for part, order in zip(self.parts, self.orders)
        ]
        self.parts = [kept for kept, _, _ in sent]
        self.sent = [message for _, message, _ in sent]
        self.flight = [arrived for _, _, arrived in sent]

    def receive(self, *others):
        zero = nothing(*others)
        self.parts = [
            part + unpacked(message, zero) for part, message in zip(self.parts, self.flight)
        ]

    def pack(self):
        self.parts = [packed(part)[None] for part in self.parts]

    def share(self, level):
        self.flight, self.sent = [], self.parts
        for part, order in zip(self.parts, self.orders):
            pairs = [(place, place ^ order[level]) for place in range(lax.axis_size(self.axis))]
            self.flight.append(lax.ppermute(part, self.axis, pairs))

    def join(self, level, *others):
        zero = nothing(*others)
        joined = []
        for part, other, order in zip(self.parts, self.flight, self.orders):
            upper = (lax.axis_index(self.axis) // order[level]) % 2
            joined.append(
                jnp.where(
                    upper.astype(jnp.float32) + zero > 0.5,
                    jnp.concatenate([other, part], axis=0),
                    jnp.concatenate([part, other], axis=0),
                )
            )
        self.parts = joined

    def result(self):
        return jnp.concatenate(
            [unpacked(part).reshape(-1, part.shape[-1]) for part in self.parts]
        )


CHUNK = 128
TILE = 256
LANES = 128
F32 = jnp.float32
BF16 = jnp.bfloat16


def mm(left, right, contract=((1,), (0,))):
    return lax.dot_general(left, right, (contract, ((), ())), preferred_element_type=F32)


NT = ((1,), (1,))
TN = ((0,), (0,))


def split(value):
    high = value.astype(BF16)
    return high, (value - high.astype(F32)).astype(BF16)


def split_three(value):
    high = value.astype(BF16)
    return (high,) + split(value - high.astype(F32))


def mm_exact(left, parts, contract=((1,), (0,))):
    return sum(mm(left, part, contract) for part in reversed(parts))


def mm_full(left, right, contract):
    pairs = ((1, 1), (2, 0), (0, 2), (1, 0), (0, 1), (0, 0))
    return sum(mm(left[i], right[j], contract) for i, j in pairs)


def logistic(value):
    return 1.0 / (1.0 + jnp.exp(-value))


def iota(shape, dim):
    return lax.broadcasted_iota(jnp.int32, shape, dim)


def triangle_sum(mask, value):
    return mm_exact(mask.astype(F32).astype(BF16), split_three(value))


def spread_pair(columns, pair):
    rows = columns.shape[0]
    first = jnp.broadcast_to(columns[:, 2 * pair : 2 * pair + 1], (rows, LANES))
    second = jnp.broadcast_to(columns[:, 2 * pair + 1 : 2 * pair + 2], (rows, LANES))
    return jnp.where(iota((rows, LANES), 1) < 64, first, second)


def spread_all(columns, width):
    return jnp.concatenate(
        [spread_pair(columns, pair) for pair in range(width // LANES)], axis=1
    )


def log_one_plus(value):
    ratio = value / (2.0 + value)
    square = ratio * ratio
    total = jnp.full_like(square, 1.0 / 15.0)
    for odd in (13, 11, 9, 7, 5, 3, 1):
        total = total * square + 1.0 / odd
    return 2.0 * ratio * total


def chunk_terms(raw, heads_row, begin, start):
    shifted = raw + heads_row[0:1]
    steps = jnp.maximum(shifted, 0.0) + log_one_plus(jnp.exp(-jnp.abs(shifted)))
    logdecay = -jnp.exp(heads_row[1:2]) * steps
    row = iota((CHUNK, CHUNK), 0)
    column = iota((CHUNK, CHUNK), 1)
    cumulative = triangle_sum(row >= column, logdecay)
    place = begin + iota((CHUNK, LANES), 0)
    segment = place >= start
    enter = begin - 1 >= start
    leave = begin + CHUNK - 1 >= start
    keep_in = jnp.where(segment == enter, 1.0, 0.0)
    keep_out = jnp.where(segment == leave, 1.0, 0.0)
    last = cumulative[CHUNK - 1 : CHUNK]
    entering = jnp.exp(cumulative) * keep_in
    leaving = jnp.exp(last - cumulative) * keep_out
    whole = jnp.exp(last) * jnp.where(enter == leave, 1.0, 0.0)
    return shifted, steps, logdecay, cumulative, entering, leaving, whole, segment


def forward_kernel(
    start_ref, rounded_ref, tail_ref, inner_ref, small_ref, taps_ref, heads_ref, gates_ref,
    pre_ref, conv_ref, kq_ref, raw_ref, local_ref, states_ref, reach_ref,
    factor_ref, final_ref, extended, state, offset,
):
    step = pl.program_id(0)
    width = gates_ref.shape[1]
    halo = tail_ref.shape[0]
    start = start_ref[0]
    low_lane = iota((CHUNK, LANES), 1) < 64

    def project(rounded):
        return mm(rounded, inner_ref[...]), mm(rounded, small_ref[...])

    @pl.when(step == 0)
    def _():
        state[...] = jnp.zeros_like(state)
        offset[...] = jnp.zeros_like(offset)
        wide, narrow = project(tail_ref[...])
        before = jnp.concatenate([wide[:, width:], narrow[:, : 2 * STATE]], axis=1)
        extended[0:halo] = before.astype(BF16).astype(F32)

    @pl.when(step > 0)
    def _():
        extended[0:halo] = extended[TILE : TILE + halo]

    wide, narrow = project(rounded_ref[...])
    gates_ref[...] = wide[:, :width]
    conv_in = jnp.concatenate([wide[:, width:], narrow[:, : 2 * STATE]], axis=1).astype(BF16)
    conv_ref[...] = conv_in
    raw_ref[...] = narrow[:, 2 * STATE :]
    extended[halo : halo + TILE] = conv_in.astype(F32)
    place = step * TILE + iota((TILE, 1), 0)
    pre = jnp.broadcast_to(taps_ref[CONV : CONV + 1], conv_in.shape)
    for tap in range(CONV):
        back = CONV - 1 - tap
        term = taps_ref[tap : tap + 1] * extended[halo - back : halo - back + TILE]
        if back:
            term = jnp.where((place >= start) & (place < start + back), 0.0, term)
        pre = pre + term
    pre_ref[...] = pre
    activated = pre * logistic(pre)
    both = activated[:, width:].astype(BF16)
    kq_ref[...] = both
    for part in range(TILE // CHUNK):
        rows = slice(part * CHUNK, (part + 1) * CHUNK)
        begin = step * TILE + part * CHUNK
        keys, queries = both[rows, :STATE], both[rows, STATE:]
        terms = chunk_terms(narrow[rows, 2 * STATE :], heads_ref[...], begin, start)
        _, steps, _, cumulative, entering, leaving, whole, segment = terms
        reach_ref[rows] = jnp.where(segment, 0.0, jnp.exp(offset[0:1] + cumulative))
        first = jnp.where(begin - 1 >= start, 0.0, 1.0)
        factor = jnp.broadcast_to(jnp.exp(offset[0:1]) * first, (8, LANES))
        factor_ref[part] = spread_all(factor, width)
        offset[...] = offset[...] + cumulative[CHUNK - 1 : CHUNK]
        held = state[...]
        states_ref[part] = held
        across = cumulative.T
        row, column = iota((CHUNK, CHUNK), 0), iota((CHUNK, CHUNK), 1)
        segment_row, segment_column = begin + row >= start, begin + column >= start
        hide = jnp.where((row >= column) & (segment_row == segment_column), 0.0, -1e30)
        scores = mm(queries, keys, NT)
        carried = mm_exact(queries, split_three(held))
        weighted = []
        for pair in range(width // LANES):
            lanes = slice(pair * LANES, (pair + 1) * LANES)
            sources = spread_pair(steps, pair) * activated[rows, lanes]
            high, low = split(sources)
            right = jnp.concatenate(
                [
                    jnp.concatenate([high, low], axis=1),
                    jnp.concatenate([high, jnp.zeros_like(low)], axis=1),
                ],
                axis=0,
            )
            left = []
            for head in (2 * pair, 2 * pair + 1):
                decay = jnp.exp(cumulative[:, head : head + 1] - across[head : head + 1] + hide)
                left.append(jnp.concatenate(split(scores * decay), axis=1))
            mixed = mm(jnp.concatenate(left, axis=0), right)
            mixed = mixed[:, :LANES] + mixed[:, LANES:]
            inner = jnp.where(low_lane, mixed[:CHUNK], mixed[CHUNK:])
            local_ref[rows, lanes] = (
                inner + spread_pair(entering, pair) * carried[:, lanes]
            )
            weighted.append(spread_pair(leaving, pair) * sources)
        added = mm_exact(keys, split_three(jnp.concatenate(weighted, axis=1)), TN)
        state[...] = spread_all(whole, width) * held + added

    @pl.when(step == pl.num_programs(0) - 1)
    def _():
        final_ref[0:STATE] = state[...]
        kept = jnp.where(pl.num_programs(0) * TILE - 1 >= start, 0.0, 1.0)
        factor = jnp.broadcast_to(jnp.exp(offset[0:1]) * kept, (8, LANES))
        final_ref[STATE : STATE + 8] = spread_all(factor, width)


def gate_kernel(
    incoming_ref, local_ref, kq_ref, reach_ref, gates_ref, pre_ref, skip_ref, cotangent_ref,
    output_ref, gain_ref, scanned_ref, back_ref, sums_ref,
):
    width = gates_ref.shape[1]
    low_lane = iota((TILE, LANES), 1) < 64
    carried = mm_exact(kq_ref[...], split_three(incoming_ref[...]))
    scanned = local_ref[...] + spread_all(reach_ref[...], width) * carried
    scanned_ref[...] = scanned
    pre = pre_ref[...]
    mixed = scanned + skip_ref[...] * (pre * logistic(pre))
    gates = gates_ref[...]
    gated = mixed * (gates * logistic(gates))
    back = mm(cotangent_ref[...].astype(BF16), output_ref[...])
    back_ref[...] = back
    squares = jnp.sum(gated * gated, axis=1, keepdims=True)
    products = jnp.sum(back * gain_ref[...] * gated, axis=1, keepdims=True)
    lane = iota((TILE, LANES), 1)
    both = jnp.where(lane == 0, squares, jnp.where(lane == 1, products, 0.0))
    sums_ref[...] = both.T[:2]


def gate_back_kernel(
    sums_ref, scanned_ref, kq_ref, reach_ref, gates_ref, pre_ref, skip_ref, back_ref, gain_ref,
    out_ref, mixed_grad_ref, gates_grad_ref, adjoint_ref, gain_grad_ref,
):
    step = pl.program_id(0)
    width = gates_ref.shape[1]
    low_lane = iota((TILE, LANES), 1) < 64

    @pl.when(step == 0)
    def _():
        adjoint_ref[...] = jnp.zeros_like(adjoint_ref)
        gain_grad_ref[...] = jnp.zeros_like(gain_grad_ref)

    sums = jnp.concatenate([sums_ref[...], jnp.zeros((LANES - 2, TILE), F32)], axis=0).T
    scale = lax.rsqrt(sums[:, 0:1] / INNER + norm_epsilon)
    shrink = scale * scale * scale * sums[:, 1:2] / INNER
    pre = pre_ref[...]
    mixed = scanned_ref[...] + skip_ref[...] * (pre * logistic(pre))
    gates = gates_ref[...]
    sigmoid = logistic(gates)
    silu = gates * sigmoid
    gated = mixed * silu
    unit = gated * scale
    back = back_ref[...]
    out_ref[...] = (unit * gain_ref[...]).astype(BF16)
    gain_grad_ref[0:1] = gain_grad_ref[0:1] + jnp.sum(back * unit, axis=0, keepdims=True)
    gated_grad = back * gain_ref[...] * scale - gated * shrink
    mixed_grad = gated_grad * silu
    mixed_grad_ref[...] = mixed_grad
    gates_grad = gated_grad * mixed * sigmoid * (1.0 + gates * (1.0 - sigmoid))
    gates_grad_ref[...] = gates_grad.astype(BF16)
    parts = split_three(spread_all(reach_ref[...], width) * mixed_grad)
    adjoint_ref[...] = adjoint_ref[...] + mm_exact(kq_ref[...], parts, TN)


def head_select(width):
    lane = iota((width, LANES), 0)
    head = iota((width, LANES), 1)
    return jnp.where((lane >= head * 64) & (lane < head * 64 + 64), 1.0, 0.0).astype(BF16)


def back_kernel(
    start_ref, pre_ref, kq_ref, raw_ref, mixed_grad_ref, scanned_ref, states_ref, factor_ref,
    incoming_ref, outgoing_ref, gates_grad_ref, skip_ref, heads_ref, taps_ref, conv_ref,
    grad_ref, steps_ref, narrow_ref, first_ref, last_ref, taps_grad_ref, heads_grad_ref, skip_grad_ref,
    extended, adjoint,
):
    step = pl.program_id(0)
    count = pl.num_programs(0)
    tile = count - 1 - step
    width = gates_grad_ref.shape[1]
    channels = pre_ref.shape[1]
    halo = first_ref.shape[0]
    start = start_ref[0]
    low_lane = iota((CHUNK, LANES), 1) < 64
    select = head_select(width)

    @pl.when(step == 0)
    def _():
        adjoint[...] = outgoing_ref[...]
        extended[TILE : TILE + halo] = jnp.zeros((halo, channels), F32)
        taps_grad_ref[...] = jnp.zeros_like(taps_grad_ref)
        heads_grad_ref[...] = jnp.zeros_like(heads_grad_ref)
        skip_grad_ref[...] = jnp.zeros_like(skip_grad_ref)

    @pl.when(step > 0)
    def _():
        extended[TILE : TILE + halo] = extended[0:halo]

    for part in reversed(range(TILE // CHUNK)):
        rows = slice(part * CHUNK, (part + 1) * CHUNK)
        begin = tile * TILE + part * CHUNK
        keys, queries = kq_ref[rows, :STATE], kq_ref[rows, STATE:]
        terms = chunk_terms(raw_ref[rows], heads_ref[...], begin, start)
        shifted, steps, logdecay, cumulative, entering, leaving, whole, _ = terms
        held = states_ref[part] + factor_ref[part, 0:1] * incoming_ref[...]
        later = adjoint[...]
        across = cumulative.T
        row, column = iota((CHUNK, CHUNK), 0), iota((CHUNK, CHUNK), 1)
        segment_row, segment_column = begin + row >= start, begin + column >= start
        hide = jnp.where((column >= row) & (segment_row == segment_column), 0.0, -1e30)
        scores = mm(keys, queries, NT)
        later_parts = split_three(later)
        held_parts = split_three(held)
        from_later = mm_exact(keys, later_parts)
        pre = pre_ref[rows]
        sigmoid = logistic(pre)
        values = pre[:, :width] * sigmoid[:, :width]
        mixed_grad = mixed_grad_ref[rows]
        scores_grad = jnp.zeros((CHUNK, CHUNK), F32)
        within, beyond, received, sent, expanded = [], [], [], [], []
        for pair in range(width // LANES):
            lanes = slice(pair * LANES, (pair + 1) * LANES)
            wide_steps = spread_pair(steps, pair)
            sources = wide_steps * values[:, lanes]
            high, low = split(sources)
            grad = mixed_grad[:, lanes]
            grad_high, grad_low = split(grad)
            right = jnp.concatenate(
                [
                    jnp.concatenate([grad_high, grad_low], axis=1),
                    jnp.concatenate([grad_high, jnp.zeros_like(grad_low)], axis=1),
                ],
                axis=0,
            )
            zero = jnp.zeros_like(high)
            highs = jnp.concatenate(
                [jnp.where(low_lane, high, zero), jnp.where(low_lane, zero, high)], axis=0
            )
            lows = jnp.concatenate(
                [jnp.where(low_lane, low, zero), jnp.where(low_lane, zero, low)], axis=0
            )
            products = (
                mm(highs, grad_high, NT) + mm(lows, grad_high, NT) + mm(highs, grad_low, NT)
            )
            left = []
            for index, head in enumerate((2 * pair, 2 * pair + 1)):
                decay = jnp.exp(across[head : head + 1] - cumulative[:, head : head + 1] + hide)
                left.append(jnp.concatenate(split(scores * decay), axis=1))
                part_rows = slice(index * CHUNK, (index + 1) * CHUNK)
                scores_grad = scores_grad + products[part_rows] * decay
            both = mm(jnp.concatenate(left, axis=0), right)
            both = both[:, :LANES] + both[:, LANES:]
            within.append(jnp.where(low_lane, both[:CHUNK], both[CHUNK:]))
            wide_leaving = spread_pair(leaving, pair)
            beyond.append(wide_leaving * from_later[:, lanes])
            sent.append(wide_leaving * sources)
            received.append(spread_pair(entering, pair) * grad)
            expanded.append(wide_steps)
        within = jnp.concatenate(within, axis=1)
        beyond = jnp.concatenate(beyond, axis=1)
        wide_steps = jnp.concatenate(expanded, axis=1)
        sent_parts = split_three(jnp.concatenate(sent, axis=1))
        received_parts = split_three(jnp.concatenate(received, axis=1))
        keys_grad = (
            sum(mm(piece, queries) for piece in reversed(split_three(scores_grad)))
            + mm_full(sent_parts, later_parts, NT)
        )
        queries_grad = (
            sum(mm(piece, keys) for piece in reversed(split_three(scores_grad.T)))
            + mm_full(received_parts, held_parts, NT)
        )
        wide_whole = spread_all(whole, width)
        adjoint[...] = wide_whole * later + mm_exact(queries, received_parts, TN)
        crossing = jnp.sum(wide_whole * held * later, axis=0, keepdims=True)
        stack = jnp.concatenate(
            [
                mixed_grad * scanned_ref[rows],
                values * within,
                values * beyond,
                jnp.broadcast_to(crossing, (8, width)),
            ],
            axis=0,
        )
        totals = sum(mm(piece, select) for piece in reversed(split_three(stack)))
        own = totals[:CHUNK]
        near = totals[CHUNK : 2 * CHUNK]
        far = totals[2 * CHUNK : 3 * CHUNK]
        crossing = totals[3 * CHUNK : 3 * CHUNK + 1]
        logdecay_grad = (
            triangle_sum(column >= row, own - steps * near)
            + triangle_sum(column < row, steps * far)
            + crossing
        )
        rate = jnp.exp(heads_ref[1:2])
        steps_grad = near + far - rate * logdecay_grad
        raw_grad = steps_grad * logistic(shifted)
        heads_grad_ref[0:1] = heads_grad_ref[0:1] + jnp.sum(raw_grad, axis=0, keepdims=True)
        heads_grad_ref[1:2] = heads_grad_ref[1:2] + jnp.sum(
            logdecay_grad * logdecay, axis=0, keepdims=True
        )
        skip_grad_ref[0:1] = skip_grad_ref[0:1] + jnp.sum(
            values * mixed_grad, axis=0, keepdims=True
        )
        values_grad = wide_steps * (within + beyond) + skip_ref[...] * mixed_grad
        activated_grad = jnp.concatenate([values_grad, keys_grad, queries_grad], axis=1)
        extended[rows] = activated_grad * sigmoid * (1.0 + pre * (1.0 - sigmoid))
        steps_ref[rows] = raw_grad.astype(BF16)

    grad_ref[:, :width] = gates_grad_ref[...]
    place = tile * TILE + iota((TILE, 1), 0)
    edge = jnp.where(start >= count * TILE, 1 << 30, start)
    conv_in = conv_ref[...].astype(F32)
    total = jnp.zeros((TILE, channels), F32)
    for tap in range(CONV):
        ahead = CONV - 1 - tap
        moved = extended[ahead : ahead + TILE]
        if ahead:
            moved = jnp.where((place < edge) & (place + ahead >= edge), 0.0, moved)
        total = total + taps_ref[tap : tap + 1] * moved
        taps_grad_ref[tap : tap + 1] = taps_grad_ref[tap : tap + 1] + jnp.sum(
            conv_in * moved, axis=0, keepdims=True
        )
    taps_grad_ref[CONV : CONV + 1] = taps_grad_ref[CONV : CONV + 1] + jnp.sum(
        extended[0:TILE], axis=0, keepdims=True
    )
    grad_ref[:, width:] = total[:, :width].astype(BF16)
    narrow_ref[...] = total[:, width:]

    @pl.when(step == 0)
    def _():
        last_ref[...] = total[TILE - halo :]

    @pl.when(step == count - 1)
    def _():
        first_ref[...] = extended[0:halo]


def rows_spec(rows, width):
    return pl.BlockSpec((rows, width), lambda step: (step, 0))


def whole_spec(shape):
    return pl.BlockSpec(shape, lambda step: (0,) * len(shape))


def like(shape, dtype=F32):
    return jax.ShapeDtypeStruct(shape, dtype)


def cost(microseconds):
    return pl.CostEstimate(
        flops=microseconds * 10**9, bytes_accessed=microseconds * 3 * 10**6, transcendentals=0
    )


def settings():
    return pltpu.CompilerParams(vmem_limit_bytes=48 * 1024 * 1024)


SCALAR = pl.BlockSpec(memory_space=pltpu.SMEM)


def forward_call(start, rounded, tail, wide, small, taps, heads):
    rows, depth = rounded.shape
    width = wide.shape[1] // 3
    channels = width + 2 * STATE
    parts = TILE // CHUNK
    return pl.pallas_call(
        forward_kernel,
        grid=(rows // TILE,),
        in_specs=[SCALAR, rows_spec(TILE, depth)]
        + [whole_spec(tail.shape), whole_spec((depth, 2 * width))]
        + [whole_spec(a.shape) for a in (small, taps, heads)],
        out_specs=[
            rows_spec(TILE, width),
            rows_spec(TILE, channels),
            rows_spec(TILE, channels),
            rows_spec(TILE, 2 * STATE),
            rows_spec(TILE, LANES),
            rows_spec(TILE, width),
            pl.BlockSpec((parts, STATE, width), lambda step: (step, 0, 0)),
            rows_spec(TILE, LANES),
            pl.BlockSpec((parts, 8, width), lambda step: (step, 0, 0)),
            whole_spec((STATE + 8, width)),
        ],
        out_shape=[
            like((rows, width)),
            like((rows, channels)),
            like((rows, channels), BF16),
            like((rows, 2 * STATE), BF16),
            like((rows, LANES)),
            like((rows, width)),
            like((rows // CHUNK, STATE, width)),
            like((rows, LANES)),
            like((rows // CHUNK, 8, width)),
            like((STATE + 8, width)),
        ],
        scratch_shapes=[
            pltpu.VMEM((TILE + tail.shape[0], channels), F32),
            pltpu.VMEM((STATE, width), F32),
            pltpu.VMEM((8, LANES), F32),
        ],
        compiler_params=settings(),
        cost_estimate=cost(33),
        name="scan_forward",
    )(start, rounded, tail, wide, small, taps, heads)


def gate_call(incoming, local, kq, reach, gates, pre, skip, cotangent, wide, gain):
    rows, width = gates.shape
    tile = rows_spec(TILE, width)
    return pl.pallas_call(
        gate_kernel,
        grid=(rows // TILE,),
        in_specs=[
            whole_spec(incoming.shape),
            tile,
            pl.BlockSpec((TILE, STATE), lambda step: (step, 1)),
            rows_spec(TILE, LANES),
            tile,
            tile,
            whole_spec(skip.shape),
            rows_spec(TILE, cotangent.shape[1]),
            pl.BlockSpec((wide.shape[0], width), lambda step: (0, 2)),
            whole_spec(gain.shape),
        ],
        out_specs=[tile, tile, pl.BlockSpec((2, TILE), lambda step: (0, step))],
        out_shape=[like((rows, width)), like((rows, width)), like((2, rows))],
        compiler_params=settings(),
        cost_estimate=cost(15),
        name="gate_forward",
    )(incoming, local, kq, reach, gates, pre, skip, cotangent, wide, gain)


def gate_back_call(sums, scanned, kq, reach, gates, pre, skip, back, gain):
    rows, width = gates.shape
    tile = rows_spec(TILE, width)
    return pl.pallas_call(
        gate_back_kernel,
        grid=(rows // TILE,),
        in_specs=[
            pl.BlockSpec((2, TILE), lambda step: (0, step)),
            tile,
            pl.BlockSpec((TILE, STATE), lambda step: (step, 1)),
            rows_spec(TILE, LANES),
            tile,
            tile,
            whole_spec(skip.shape),
            tile,
            whole_spec(gain.shape),
        ],
        out_specs=[tile, tile, tile, whole_spec((STATE, width)), whole_spec((8, width))],
        out_shape=[
            like((rows, width), BF16),
            like((rows, width)),
            like((rows, width), BF16),
            like((STATE, width)),
            like((8, width)),
        ],
        compiler_params=settings(),
        cost_estimate=cost(12),
        name="gate_backward",
    )(sums, scanned, kq, reach, gates, pre, skip, back, gain)


def back_call(
    start, pre, kq, raw, mixed_grad, scanned, states, factor, incoming, outgoing, gates_grad, skip,
    heads, taps, conv_in,
):
    rows, width = gates_grad.shape
    channels = pre.shape[1]
    count = rows // TILE
    parts = TILE // CHUNK

    def tile(columns):
        return pl.BlockSpec((TILE, columns), lambda step: (count - 1 - step, 0))

    def blocks(height):
        return pl.BlockSpec((parts, height, width), lambda step: (count - 1 - step, 0, 0))

    return pl.pallas_call(
        back_kernel,
        grid=(count,),
        in_specs=[
            SCALAR,
            tile(channels),
            tile(2 * STATE),
            tile(LANES),
            tile(width),
            tile(width),
            blocks(STATE),
            blocks(8),
            whole_spec(incoming.shape),
            whole_spec(outgoing.shape),
            tile(width),
            whole_spec(skip.shape),
            whole_spec(heads.shape),
            whole_spec(taps.shape),
            tile(channels),
        ],
        out_specs=[
            tile(2 * width),
            tile(LANES),
            tile(2 * STATE),
            whole_spec((16, channels)),
            whole_spec((16, channels)),
            whole_spec((8, channels)),
            whole_spec((8, LANES)),
            whole_spec((8, width)),
        ],
        out_shape=[
            like((rows, 2 * width), BF16),
            like((rows, LANES), BF16),
            like((rows, 2 * STATE)),
            like((16, channels)),
            like((16, channels)),
            like((8, channels)),
            like((8, LANES)),
            like((8, width)),
        ],
        scratch_shapes=[
            pltpu.VMEM((TILE + 16, channels), F32),
            pltpu.VMEM((STATE, width), F32),
        ],
        compiler_params=settings(),
        cost_estimate=cost(48),
        name="scan_backward",
    )(
        start, pre, kq, raw, mixed_grad, scanned, states, factor, incoming, outgoing, gates_grad,
        skip, heads, taps, conv_in,
    )


def adamw(weight, gradient, first, second, rate, shrink):
    first_new = moment_decay * first + (1.0 - moment_decay) * gradient
    second_new = moment_decay * second + (1.0 - moment_decay) * gradient * gradient
    correction = 1.0 - moment_decay**STEP
    ratio = first_new / correction / (jnp.sqrt(second_new / correction) + adam_epsilon)
    return (weight - rate * (ratio + shrink * weight), first_new, second_new)


def on_device(
    tokens,
    cotangent,
    sequence_starts,
    norm_gain,
    inner_weight,
    state_weight,
    step_weight,
    inner_params,
    state_conv,
    head_params,
    output_weight,
    first_norm_gain,
    second_norm_gain,
    first_inner_weight,
    second_inner_weight,
    first_state_weight,
    second_state_weight,
    first_step_weight,
    second_step_weight,
    first_inner_params,
    second_inner_params,
    first_state_conv,
    second_state_conv,
    first_head_params,
    second_head_params,
    first_output_weight,
    second_output_weight,
):
    rows, width = tokens.shape
    inner_local = inner_weight.shape[2]
    state_local = state_weight.shape[2]
    heads_local = step_weight.shape[1]
    head_place = lax.axis_index("head")
    start = sequence_starts[0]
    channels = inner_local + 2 * STATE
    split_two = 2 * inner_local
    wide = jnp.concatenate([inner_weight.reshape(-1, split_two), output_weight.T], axis=1)
    wide = lax.all_gather(wide.astype(jnp.bfloat16), "seq", axis=0, tiled=True)
    inner_full, output_full = wide[:, :split_two], wide[:, split_two:]
    own_rows = state_weight.shape[0]
    side = jnp.concatenate(
        [
            state_weight.reshape(own_rows, 2, state_local),
            state_conv,
            jnp.zeros((3, 2, state_local), jnp.float32),
        ],
        axis=0,
    )
    side = lax.all_gather(side.reshape(own_rows + 8, 2 * state_local), "head")
    side = side.reshape(-1, own_rows + 8, 2, state_local).transpose(1, 2, 0, 3)
    side = side.reshape(own_rows + 8, 2 * STATE)
    narrow = jnp.concatenate(
        [side[:own_rows], step_weight, jnp.zeros((own_rows, LANES - heads_local), jnp.float32)],
        axis=1,
    )
    small_full = lax.all_gather(narrow.astype(jnp.bfloat16), "seq", axis=0, tiled=True)
    taps = jnp.concatenate([inner_params[: CONV + 1], side[own_rows : own_rows + CONV + 1]], axis=1)
    taps = jnp.pad(taps, ((0, 8 - CONV - 1), (0, 0)))
    heads = jnp.pad(head_params[:2], ((0, 6), (0, LANES - heads_local)))
    skip = jnp.repeat(head_params[2], inner_local // heads_local)[None]
    gate_gain = inner_params[CONV + 1 : CONV + 2]
    places = jnp.arange(rows - 16, rows, dtype=jnp.int32)
    tail_keep = ((places >= start) == (start <= rows - 1))[:, None]
    recent = (jnp.arange(16) >= 16 - CONV + 1)[:, None]
    tail = passed_along(jnp.where(tail_keep & recent, tokens[rows - 16 :], 0.0), "seq", 1)
    inverse = lax.rsqrt(jnp.mean(tokens * tokens, axis=1, keepdims=True) + norm_epsilon)
    rounded = (tokens * inverse * norm_gain).astype(jnp.bfloat16)
    tail_scale = lax.rsqrt(jnp.mean(tail * tail, axis=1, keepdims=True) + norm_epsilon)
    tail = (tail * tail_scale * norm_gain).astype(jnp.bfloat16)
    begin = start[None]
    (
        gates, pre, conv_in, kq, raw, local, states, reach, factor, final
    ) = forward_call(
        begin, rounded, tail, wide, small_full, taps, heads
    )
    incoming = carried_in(final, "seq", False)
    scanned, back, sums = gate_call(
        incoming, local, kq, reach, gates, pre, skip, cotangent, wide, gate_gain
    )
    sums = lax.psum(sums, "head")
    gate_out, mixed_grad, gates_grad, adjoint, gain_grad = gate_back_call(
        sums, scanned, kq, reach, gates, pre, skip, back, gate_gain
    )
    outgoing = carried_in(jnp.concatenate([adjoint, final[STATE:]], axis=0), "seq", True)
    partial_out = lax.dot_general(
        gate_out, output_full, (((1,), (1,)), ((), ())), preferred_element_type=jnp.float32
    )
    branch = LineSum(partial_out, "head")
    branch.send(0)
    output_weight_grad = lax.dot_general(
        cotangent.astype(jnp.bfloat16),
        gate_out,
        (((0,), (0,)), ((), ())),
        preferred_element_type=jnp.float32,
    )
    output_total = lax.psum_scatter(output_weight_grad, "seq", scatter_dimension=0, tiled=True)
    outgoing = outgoing + nothing(output_weight_grad, *branch.sent)
    (
        wide_grad, step_grad, narrow_grad, first_grad, last_grad, taps_grad, heads_grad, skip_grad
    ) = back_call(
        begin, pre, kq, raw, mixed_grad, scanned, states, factor, incoming, outgoing, gates_grad,
        skip, heads, taps, conv_in,
    )
    output_total = (output_total + nothing(first_grad)).T
    branch.receive(first_grad)
    branch.send(1)
    early = (jnp.arange(8) < jnp.minimum(start, CONV - 1))[:, None]
    halo = passed_along(jnp.where(early, first_grad[:8], 0.0), "seq", -1)
    ahead_rows = jnp.concatenate([jnp.zeros((16, channels), jnp.float32), halo], axis=0)
    last_conv = conv_in[rows - 16 :].astype(jnp.float32)
    extra = []
    for tap in range(CONV - 1):
        ahead = CONV - 1 - tap
        moved = jnp.where(tail_keep, ahead_rows[ahead : ahead + 16], 0.0)
        last_grad = last_grad + taps[tap] * moved
        extra.append(jnp.sum(last_conv * moved, axis=0))
    taps_grad = taps_grad[: CONV + 1] + jnp.pad(jnp.stack(extra), ((0, 2), (0, 0)))
    wide_grad = lax.dynamic_update_slice(
        wide_grad, last_grad[:, :inner_local].astype(jnp.bfloat16), (rows - 16, inner_local)
    )
    narrow_grad = lax.dynamic_update_slice(narrow_grad, last_grad[:, inner_local:], (rows - 16, 0))
    head_count = lax.axis_size("head")
    piece = rows // (2 * head_count)
    narrow_grad = narrow_grad.reshape(2, head_count, piece, 2 * STATE)
    narrow_grad = jnp.stack(
        [
            narrow_grad[0, jnp.array([reversed_bits(z, head_count) for z in range(head_count)])],
            narrow_grad[1],
        ],
        axis=1,
    )
    state_grad = lax.psum_scatter(
        narrow_grad.reshape(rows, 2 * STATE), "head", scatter_dimension=0, tiled=True
    ).astype(jnp.bfloat16)
    own_rows = [
        reversed_bits(head_place, head_count) * piece,
        rows // 2 + head_place * piece,
    ]
    own_rounded = jnp.concatenate(
        [lax.dynamic_slice_in_dim(rounded, first, piece, 0) for first in own_rows]
    )
    normed_part = lax.dot_general(
        wide_grad,
        inner_full,
        (((1,), (1,)), ((), ())),
        preferred_element_type=jnp.float32,
    ) + lax.dot_general(
        step_grad,
        small_full[:, 2 * STATE :],
        (((1,), (1,)), ((), ())),
        preferred_element_type=jnp.float32,
    )
    normed_state = lax.dot_general(
        state_grad,
        small_full[:, : 2 * STATE],
        (((1,), (1,)), ((), ())),
        preferred_element_type=jnp.float32,
    )
    state_matrix = lax.dot_general(
        own_rounded, state_grad, (((0,), (0,)), ((), ())), preferred_element_type=jnp.float32
    )
    matrix_grad = lax.dot_general(
        rounded,
        jnp.concatenate(
            [
                wide_grad,
                step_grad[:, :heads_local],
            ],
            axis=1,
        ),
        (((0,), (0,)), ((), ())),
        preferred_element_type=jnp.float32,
    )
    matrix_grad = jnp.concatenate([state_matrix, matrix_grad], axis=1)
    own_tokens = jnp.concatenate(
        [lax.dynamic_slice_in_dim(tokens * inverse, first, piece, 0) for first in own_rows]
    )
    norm_gain_grad = jnp.sum(normed_part * tokens * inverse, axis=0) + jnp.sum(
        normed_state * own_tokens, axis=0
    )
    normed = LineSum(normed_part, "head")
    normed.send(0)
    for level in range(1, branch.levels):
        branch.receive(*normed.sent)
        if level < branch.levels - 1:
            branch.send(level + 1)
    branch.pack()
    branch.share(branch.levels - 1)
    matrix_total = lax.psum_scatter(matrix_grad, "seq", scatter_dimension=0, tiled=True)
    normed.receive(*branch.sent)
    for level in range(1, normed.levels):
        normed.send(level)
        if level < normed.levels - 1:
            normed.receive()
    shared = jnp.concatenate(
        [norm_gain_grad.reshape(-1, LANES), taps_grad[:, inner_local:].reshape(-1, LANES)], axis=0
    )
    shared = shared + nothing(*normed.sent)
    gain_rows = width // LANES
    own_gain = jnp.concatenate([taps_grad[:, :inner_local], gain_grad[:1]], axis=0)
    skip_sums = jnp.sum(skip_grad[0].reshape(heads_local, -1), axis=1)
    head_rows = jnp.concatenate([heads_grad[:2], jnp.pad(skip_sums, (0, LANES - heads_local))[None]])
    totals = lax.psum(
        jnp.concatenate([shared, own_gain.reshape(-1, LANES), head_rows], axis=0), "seq"
    )
    shared_rows = gain_rows + 2 * (CONV + 1)
    for level in reversed(range(1, branch.levels)):
        branch.join(level, matrix_grad, *normed.sent)
        branch.share(level - 1)
    normed.receive(totals, *branch.sent)
    normed.parts = [part + more for part, more in zip(normed.parts, jnp.split(normed_state, 2))]
    normed.pack()
    own_rows = matrix_total.shape[0]
    over_heads = lax.psum(
        jnp.concatenate(
            [
                matrix_total[:, : 2 * STATE],
                jnp.pad(totals[:shared_rows].reshape(-1, 2 * STATE), ((0, 7), (0, 0))),
            ],
            axis=0,
        ),
        "head",
    )
    state_total = over_heads[:own_rows].reshape(-1, 2, STATE)
    shared = over_heads[own_rows : own_rows + shared_rows // 2].reshape(shared_rows, LANES)
    normed.share(normed.levels - 1)
    for level in reversed(range(1, normed.levels)):
        normed.join(level, matrix_total)
        normed.share(level - 1)
    branch.join(0, *normed.sent)
    output = tokens + branch.result()
    normed.join(0)
    normed_grad = normed.result()
    scaled_grad = normed_grad * norm_gain
    input_gradient = (
        cotangent
        + inverse * scaled_grad
        - tokens * inverse**3 * jnp.mean(scaled_grad * tokens, axis=1, keepdims=True)
    )
    state_total = lax.dynamic_slice_in_dim(state_total, head_place * state_local, state_local, 2)
    matrix_total = matrix_total[:, 2 * STATE :]
    inner_total = matrix_total[:, :split_two].reshape(-1, 2, inner_local)
    step_total = matrix_total[:, split_two:]
    gain_total = shared[:gain_rows].reshape(-1)
    conv_total = lax.dynamic_slice_in_dim(
        shared[gain_rows:].reshape(CONV + 1, 2, STATE),
        head_place * state_local,
        state_local,
        2,
    )
    params_total = totals[shared_rows:-3].reshape(CONV + 2, inner_local)
    head_sum = totals[-3:, :heads_local]
    matrix_rate = 2.0 * D ** (-0.5)
    output_rate = 2.0 * INNER ** (-0.5)
    gain_next = adamw(norm_gain, gain_total, first_norm_gain, second_norm_gain, 0.5, 0.0)
    inner_next = adamw(
        inner_weight,
        inner_total,
        first_inner_weight,
        second_inner_weight,
        matrix_rate,
        weight_decay,
    )
    state_next = adamw(
        state_weight,
        state_total,
        first_state_weight,
        second_state_weight,
        matrix_rate,
        weight_decay,
    )
    step_next = adamw(
        step_weight, step_total, first_step_weight, second_step_weight, matrix_rate, weight_decay
    )
    params_next = adamw(
        inner_params, params_total, first_inner_params, second_inner_params, 0.5, 0.0
    )
    conv_next = adamw(state_conv, conv_total, first_state_conv, second_state_conv, 0.5, 0.0)
    head_next = adamw(head_params, head_sum, first_head_params, second_head_params, 3.0, 0.0)
    output_next = adamw(
        output_weight,
        output_total,
        first_output_weight,
        second_output_weight,
        output_rate,
        weight_decay,
    )
    return (
        output,
        input_gradient,
        gain_next[0],
        gain_next[1],
        gain_next[2],
        inner_next[0],
        inner_next[1],
        inner_next[2],
        state_next[0],
        state_next[1],
        state_next[2],
        step_next[0],
        step_next[1],
        step_next[2],
        params_next[0],
        params_next[1],
        params_next[2],
        conv_next[0],
        conv_next[1],
        conv_next[2],
        head_next[0],
        head_next[1],
        head_next[2],
        output_next[0],
        output_next[1],
        output_next[2],
    )


def solution(mesh):
    placed = (
        P("seq", None),
        P("seq", None),
        P("seq"),
        P(),
        P("seq", None, "head"),
        P("seq", None, "head"),
        P("seq", "head"),
        P(None, "head"),
        P(None, None, "head"),
        P(None, "head"),
        P("head", "seq"),
        P(),
        P(),
        P("seq", None, "head"),
        P("seq", None, "head"),
        P("seq", None, "head"),
        P("seq", None, "head"),
        P("seq", "head"),
        P("seq", "head"),
        P(None, "head"),
        P(None, "head"),
        P(None, None, "head"),
        P(None, None, "head"),
        P(None, "head"),
        P(None, "head"),
        P("head", "seq"),
        P("head", "seq"),
    )
    return jax.shard_map(
        on_device,
        mesh=mesh,
        in_specs=placed,
        out_specs=(
            P("seq", None),
            P("seq", None),
            P(),
            P(),
            P(),
            P("seq", None, "head"),
            P("seq", None, "head"),
            P("seq", None, "head"),
            P("seq", None, "head"),
            P("seq", None, "head"),
            P("seq", None, "head"),
            P("seq", "head"),
            P("seq", "head"),
            P("seq", "head"),
            P(None, "head"),
            P(None, "head"),
            P(None, "head"),
            P(None, None, "head"),
            P(None, None, "head"),
            P(None, None, "head"),
            P(None, "head"),
            P(None, "head"),
            P(None, "head"),
            P("head", "seq"),
            P("head", "seq"),
            P("head", "seq"),
        ),
        check_vma=False,
    )
```
